256 devices in a mesh: island: 16 (over z_hi, x, core), fsdp: 16 (over z_lo, y).
Axes of the slice: x: 4, y: 4, z: 8 (z_hi: 2, z_lo: 4; z = z_hi * 4 + z_lo), core: 2. Of those that a mesh axis runs over, the one named last changes fastest.
Arguments:
- tokens: bfloat16 [16, 2048, 3072], P('island', 'fsdp'), may hold values from -6 to 6
- routing: int32 [16, 2048, 2], P('island', 'fsdp'), may hold values from 0 to 7, as said below
- router_weight: bfloat16 [16, 2048, 2], P('island', 'fsdp'), may hold values from 0.19921875 to 1
- w_up: bfloat16 [16, 3072, 8192], P('island', None, 'fsdp'), may hold values from -5 to 5
- w_down: bfloat16 [16, 8192, 3072], P('island', 'fsdp'), may hold values from -5 to 5
- step_number: int32 [1], replicated, may hold values from 0 to 3999
Outputs:
- new_up: bfloat16 [16, 3072, 8192], P('island', None, 'fsdp')
- new_down: bfloat16 [16, 8192, 3072], P('island', 'fsdp')
The draws below stay inside these ranges and needn't reach their ends.
Inputs may be any that keep to these rules, and one draw needn't show every extreme that they name: `routing`: each row names 2 different experts. In each aligned block of 128 rows (the rows of one device) at most 40 rows name expert 0, at least 20 do, and some block has exactly 40.
All inputs are finite; a program needn't handle non-finite values.
Results may differ from the reference program's by a relative error of at most 0.006.
Values may be sent and summed in bfloat16 or wider, within the bound.
A program may use at most 128 MiB of HBM per device.

```python
import jax
import jax.numpy as jnp
from jax import lax

D = 3072
FF = 8192
N_EXP = 8
TOP = 2
TOK_DEV = 128
CAP = 40
TOK_ISL = 2048
BITS = 4
N_ISLAND = 16
N_FSDP = 16


def draw_routing(key, part):
    block_count = N_ISLAND * N_FSDP
    count_key, forced_key, order_key, first_key, second_key, flip_key = jax.random.split(key, 6)
    per_block = jax.random.randint(count_key, (block_count,), CAP // 2, CAP + 1)
    forced = jax.random.randint(forced_key, (), 0, block_count)
    per_block = jnp.where(jnp.arange(block_count) == forced, CAP, per_block)
    rank_rows = jax.vmap(lambda one_key: jax.random.permutation(one_key, TOK_DEV))(jax.random.split(order_key, block_count))
    routed = rank_rows < per_block[:, None]
    first_pick = jax.random.randint(first_key, (block_count, TOK_DEV), 1, N_EXP)
    offset = jax.random.randint(second_key, (block_count, TOK_DEV), 1, N_EXP - 1)
    second_pick = 1 + (first_pick - 1 + offset) % (N_EXP - 1)
    flipped = jax.random.randint(flip_key, (block_count, TOK_DEV), 0, 2) == 1
    column_a = jnp.where(routed, jnp.where(flipped, first_pick, 0), first_pick)
    column_b = jnp.where(routed, jnp.where(flipped, 0, first_pick), second_pick)
    stacked = jnp.stack([column_a, column_b], axis=-1)
    return stacked.reshape(N_ISLAND, N_FSDP * TOK_DEV, 2).astype(jnp.int32)


def steps_of(stream_key, shape, cuts, low, largest):
    loudness, own = 1.0, jax.random.fold_in(stream_key, 6)
    for axis_at, parts in cuts:
        draws = jnp.exp(jax.random.uniform(jax.random.fold_in(own, axis_at), (parts,), jnp.float32, low / len(cuts), largest / len(cuts)))
        loudness = loudness * jnp.repeat(draws, shape[axis_at] // parts).reshape([-1 if axis == axis_at else 1 for axis in range(len(shape))])
    return loudness


def scatter_about(rng, extent, scale, reach, cuts=(), kind=jnp.bfloat16):
    drawn = jax.random.normal(rng, extent, jnp.float32) * scale
    if len(cuts) > 0:
        drawn = steps_of(rng, extent, cuts, -0.22, 0.18) * drawn
    return jnp.clip(drawn, min=-reach, max=reach).astype(kind)


def setup_inputs(seed: int = 0) -> dict:
    seeds = jax.random.split(jax.random.key(seed), 7)
    tokens = scatter_about(seeds[0], (N_ISLAND, TOK_ISL, D), 1.0, 6.0, ((0, 16), (1, 16)))
    routing = draw_routing(jax.random.fold_in(seeds[6], 71), 0)
    router_weight = jnp.clip(0.19921875 + 0.80078125 * jax.random.uniform(seeds[2], (N_ISLAND, TOK_ISL, TOP), jnp.float32) ** steps_of(seeds[2], (N_ISLAND, TOK_ISL, TOP), ((0, 16), (1, 16)), -0.2, 0.2), 0.19921875, 1.0).astype(jnp.bfloat16)
    w_up = scatter_about(seeds[3], (N_ISLAND, D, FF), 1.0, 5.0, ((0, 16), (2, 16)))
    w_down = scatter_about(seeds[4], (N_ISLAND, FF, D), 1.0, 5.0, ((0, 16), (1, 16)))
    step_number = jax.random.randint(seeds[5], (1,), 0, 1000 * BITS).astype(jnp.int32)
    return dict(tokens=tokens, routing=routing, router_weight=router_weight, w_up=w_up, w_down=w_down, step_number=step_number)


learn_rate = 4.0


def silu_slope(values):
    sig = jax.nn.sigmoid(values)
    return sig * (1.0 + values * (1.0 - sig))


def dispatch(block_rows, block_routes, block_weight):
    is_target = block_routes == 0
    chosen = jnp.any(is_target, axis=1)
    route_share = jnp.sum(jnp.where(is_target, block_weight.astype(jnp.float32), jnp.float32(0.0)), axis=1)
    slot_index = jnp.cumsum(chosen.astype(jnp.int32)) - 1
    slot_table = (slot_index[None, :] == jnp.arange(CAP, dtype=jnp.int32)[:, None]) & chosen[None, :]
    slot_rows = jnp.dot(slot_table.astype(jnp.bfloat16), block_rows, preferred_element_type=jnp.float32).astype(jnp.bfloat16)
    slot_share = jnp.dot(slot_table.astype(jnp.float32), route_share, precision=lax.Precision.HIGHEST)
    return slot_rows, slot_share


def island_step(operands):
    island_tokens, island_routes, island_weight, up_matrix, down_matrix = operands
    slot_rows, slot_share = jax.vmap(dispatch)(
        island_tokens.reshape(N_FSDP, TOK_DEV, D),
        island_routes.reshape(N_FSDP, TOK_DEV, TOP),
        island_weight.reshape(N_FSDP, TOK_DEV, TOP))
    slot_rows = slot_rows.reshape(N_FSDP * CAP, D)
    slot_share = slot_share.reshape(N_FSDP * CAP, 1)
    scale_up = D ** -0.5
    scale_down = FF ** -0.5
    pre_act = scale_up * jnp.dot(slot_rows, up_matrix, preferred_element_type=jnp.float32)
    hidden = jax.nn.silu(pre_act).astype(jnp.bfloat16)
    expert_out = scale_down * jnp.dot(hidden, down_matrix, preferred_element_type=jnp.float32)
    errors = (slot_share * (slot_share * expert_out - slot_rows.astype(jnp.float32))).astype(jnp.bfloat16)
    grad_down = scale_down * jnp.dot(hidden.T, errors, preferred_element_type=jnp.float32)
    grad_hidden = scale_down * jnp.dot(errors, down_matrix.T, preferred_element_type=jnp.float32)
    grad_pre = (grad_hidden * silu_slope(pre_act)).astype(jnp.bfloat16)
    grad_up = scale_up * jnp.dot(slot_rows.T, grad_pre, preferred_element_type=jnp.float32)
    moved_up = (up_matrix.astype(jnp.float32) - learn_rate * grad_up).astype(jnp.bfloat16)
    moved_down = (down_matrix.astype(jnp.float32) - learn_rate * grad_down).astype(jnp.bfloat16)
    return moved_up, moved_down


def reference(tokens, routing, router_weight, w_up, w_down, step_number):
    moved_up, moved_down = lax.map(island_step, (tokens, routing, router_weight, w_up, w_down))
    bit_index = jnp.remainder(step_number[0].astype(jnp.int32), jnp.int32(BITS))
    partner = jnp.bitwise_xor(jnp.arange(N_ISLAND, dtype=jnp.int32), jnp.left_shift(jnp.int32(1), bit_index))
    other_up = jnp.take(moved_up, partner, axis=0)
    other_down = jnp.take(moved_down, partner, axis=0)
    new_up = (0.5 * (moved_up.astype(jnp.float32) + other_up.astype(jnp.float32))).astype(jnp.bfloat16)
    new_down = (0.5 * (moved_down.astype(jnp.float32) + other_down.astype(jnp.float32))).astype(jnp.bfloat16)
    return new_up, new_down
```

```python
from functools import partial

import jax
import jax.numpy as jnp
from jax import lax
from jax.experimental import pallas as pl
from jax.experimental.pallas import tpu as pltpu
from jax.sharding import PartitionSpec as P

MESH = pl.DeviceIdType.MESH
F32, BF16 = jnp.float32, jnp.bfloat16
CAP = 40
PAIR = 2 * CAP
STAGE = 48
SIDE = 4
GROUP = SIDE * PAIR
LANES = 128

learn_rate = 4.0


def silu_slope(values):
    sig = jax.nn.sigmoid(values)
    return sig * (1.0 + values * (1.0 - sig))


def unit(ref, yy, zz, low=0, size=None):
    start = pl.multiple_of(((yy // 2) * SIDE + zz) * PAIR, 16)
    size = ref.shape[-1] if size is None else size
    return ref.at[yy % 2, pl.ds(start, PAIR), pl.ds(low, size)]


def place():
    me = lax.axis_index("fsdp")
    return me // SIDE, me % SIDE


def across(z, k):
    return (z, z + 1 - 2 * (z % 2), (z + 2) % SIDE, SIDE - 1 - z)[k]


class Sender:
    def __init__(self):
        self.started = []

    def send(self, src, dst, send_sem, recv_sem, device):
        copy = pltpu.make_async_remote_copy(
            src_ref=src,
            dst_ref=dst,
            send_sem=send_sem,
            recv_sem=recv_sem,
            device_id=device,
            device_id_type=MESH,
        )
        copy.start()
        self.started.append(copy)

    def drain(self):
        for copy in self.started:
            copy.wait_send()
        self.started = []


def arrived(dst, sems, recv_sem, device):
    pltpu.make_async_remote_copy(
        src_ref=dst, dst_ref=dst, send_sem=sems, recv_sem=recv_sem, device_id=device, device_id_type=MESH
    ).wait_recv()


def at(zz, yy):
    return {"fsdp": zz * SIDE + yy}


class Gather:
    def __init__(self, buf, send_sem, full_sem, half_sem, out):
        self.buf, self.send_sem, self.full_sem, self.half_sem, self.out = buf, send_sem, full_sem, half_sem, out
        self.z, self.y = place()
        self.part = buf.shape[-1] // 2

    def wait_full(self, yy, zz):
        view = unit(self.buf, yy, zz)
        arrived(view, self.send_sem.at[0], self.full_sem.at[yy * SIDE + zz], at(self.z, (self.y + 1) % SIDE))

    def push(self, k):
        z, y = self.z, self.y
        zz = across(z, k)
        if k > 0:
            self.wait_full(y, zz)
        view = unit(self.buf, y, zz)
        for i, step in enumerate((1, SIDE - 1)):
            self.out.send(
                view, view, self.send_sem.at[3 + 2 * k + i], self.full_sem.at[y * SIDE + zz], at(z, (y + step) % SIDE)
            )

    def forward(self, k):
        z, y = self.z, self.y
        zz = across(z, k)
        for i, step in enumerate((1, SIDE - 1)):
            source = (y + SIDE - step) % SIDE
            self.wait_full(source, zz)
            view = unit(self.buf, source, zz, i * self.part, self.part)
            self.out.send(
                view,
                view,
                self.send_sem.at[11 + 2 * k + i],
                self.half_sem.at[i, source * SIDE + zz],
                at(z, (y + step) % SIDE),
            )

    def run(self):
        z, y = self.z, self.y
        own = unit(self.buf, y, z)
        for k in (3, 2, 1):
            self.out.send(own, own, self.send_sem.at[k - 1], self.full_sem.at[y * SIDE + z], at(across(z, k), y))
        for k in range(SIDE):
            self.push(k)
            if k > 0:
                self.forward(k - 1)
        self.forward(SIDE - 1)

    def finish(self):
        z, y = self.z, self.y
        far = (y + 2) % SIDE
        for k in range(SIDE):
            zz = across(z, k)
            for i in range(2):
                view = unit(self.buf, far, zz, i * self.part, self.part)
                arrived(view, self.send_sem.at[0], self.half_sem.at[i, far * SIDE + zz], at(z, (y + 1) % SIDE))


def expert_kernel(
    scale_up,
    scale_down,
    tokens,
    routes,
    weights,
    up_hbm,
    down_hbm,
    slots_out,
    errors_out,
    pre_out,
    slots,
    errors,
    up,
    down,
    pre,
    hidden,
    part,
    got_half,
    got_full,
    got_z,
    total,
    stage_out,
    stage_in,
    share_col,
    load_sem,
    store_sem,
    stage_sem,
    gather_send,
    gather_full,
    gather_half,
    sum_send,
    sum_half,
    sum_full,
    sum_z,
):
    z, y = place()
    half = tokens.shape[1] // 2
    quarter = half // 2
    out = Sender()
    y_up, y_down, y_far = (y + 1) % SIDE, (y + SIDE - 1) % SIDE, (y + 2) % SIDE
    y_pair = y + 1 - 2 * (y % 2)

    loads = [
        pltpu.make_async_copy(up_hbm, up, load_sem.at[0]),
        pltpu.make_async_copy(down_hbm, down, load_sem.at[1]),
    ]
    for load in loads:
        load.start()
    barrier = pltpu.get_barrier_semaphore()
    peers = [at(across(z, k), y) for k in (1, 2, 3)] + [at(z, y_up), at(z, y_down)]
    for peer in peers:
        pl.semaphore_signal(barrier, inc=1, device_id=peer, device_id_type=MESH)

    target0 = routes[0:1, :] == 0
    target1 = routes[1:2, :] == 0
    chosen = (target0 | target1).astype(F32)
    share_row = jnp.where(target0, weights[0:1, :], 0.0) + jnp.where(target1, weights[1:2, :], 0.0)
    count = chosen.shape[1]
    earlier = lax.broadcasted_iota(jnp.int32, (count, count), 0) <= lax.broadcasted_iota(jnp.int32, (count, count), 1)
    ranks = jnp.dot(
        jnp.broadcast_to(chosen, (8, count)).astype(BF16), earlier.astype(BF16), preferred_element_type=F32
    )[0:1, :]
    slot_ids = lax.broadcasted_iota(jnp.int32, (STAGE, count), 0).astype(F32)
    takes = (slot_ids == ranks - 1.0) & (chosen > 0.0) & (slot_ids < float(CAP))
    table = jnp.where(takes, 1.0, 0.0).astype(BF16)
    own_share = jnp.sum(jnp.where(takes, share_row, 0.0), axis=1, keepdims=True)
    mine = y % 2
    own_rows = jnp.dot(
        table, tokens[:, pl.ds(pl.multiple_of(mine * half, LANES), half)], preferred_element_type=F32
    )
    stage_out[:, 0:half] = jnp.dot(
        table, tokens[:, pl.ds(pl.multiple_of((1 - mine) * half, LANES), half)], preferred_element_type=F32
    ).astype(BF16)
    stage_out[:, half:] = jnp.broadcast_to(own_share, (STAGE, LANES)).astype(BF16)
    pl.semaphore_wait(barrier, len(peers))
    out.send(stage_out, stage_in, stage_sem.at[0], stage_sem.at[1], at(z, y_pair))
    arrived(stage_in, stage_sem.at[0], stage_sem.at[1], at(z, y_pair))
    other_rows = stage_in[:, 0:half].astype(F32)
    other_share = stage_in[:, half:].astype(F32)[0:CAP, 0:1]
    first = mine == 0
    own_rows, own_share, other_rows = own_rows[0:CAP], own_share[0:CAP], other_rows[0:CAP]
    rows = jnp.concatenate(
        [jnp.where(first, own_rows, other_rows), jnp.where(first, other_rows, own_rows)], axis=0
    ).astype(BF16)
    unit(slots, y, z)[...] = rows
    share_col[...] = jnp.broadcast_to(
        jnp.concatenate(
            [jnp.where(first, own_share, other_share), jnp.where(first, other_share, own_share)], axis=0
        ),
        (PAIR, LANES),
    )

    spread = Gather(slots, gather_send.at[0], gather_full.at[0], gather_half.at[0], out)
    spread.run()

    def ahead(group):
        begin = pl.multiple_of(group * GROUP, 16)
        block = pl.ds(begin, GROUP)
        values = scale_up * (
            jnp.dot(slots[0, block, :], up[0:half, :], preferred_element_type=F32)
            + jnp.dot(slots[1, block, :], up[half:, :], preferred_element_type=F32)
        )
        pre[block, :] = values
        hidden[block, :] = jax.nn.silu(values).astype(BF16)

    for load in loads:
        load.wait()
    ahead(y // 2)
    spread.finish()
    ahead(1 - y // 2)
    stores = [
        pltpu.make_async_copy(slots.at[0], slots_out.at[:, 0:half], store_sem.at[0]),
        pltpu.make_async_copy(slots.at[1], slots_out.at[:, half : 2 * half], store_sem.at[1]),
        pltpu.make_async_copy(pre, pre_out, store_sem.at[2]),
    ]
    for store in stores:
        store.start()

    def column(yy):
        begin = pl.multiple_of((yy // 2) * GROUP, 16)
        block = pl.ds(begin, GROUP)
        side = yy % 2
        width = half // 3
        for j in range(3):
            part[side, block, j * width : (j + 1) * width] = (
                scale_down
                * jnp.dot(
                    hidden[block, :],
                    down[:, pl.ds(pl.multiple_of(side * half + j * width, LANES), width)],
                    preferred_element_type=F32,
                )
            ).astype(BF16)

    column(y_far)
    for zz in range(SIDE):
        for i, target in enumerate((y_down, y_up)):
            out.send(
                unit(part, y_far, zz, i * quarter, quarter),
                got_half.at[i, zz],
                sum_send.at[2 * zz + i],
                sum_half.at[i, zz],
                at(z, target),
            )
    column(y_down)
    column(y_up)
    for zz in range(SIDE):
        for i, target in enumerate((y_down, y_up)):
            arrived(got_half.at[i, zz], sum_send.at[0], sum_half.at[i, zz], at(z, target))
            view = unit(part, target, zz, i * quarter, quarter)
            view[...] = (view[...].astype(F32) + got_half[i, zz].astype(F32)).astype(BF16)
            out.send(
                unit(part, target, zz),
                got_full.at[i, zz],
                sum_send.at[8 + 2 * zz + i],
                sum_full.at[i, zz],
                at(z, target),
            )
    column(y)
    for k in (3, 2, 1, 0):
        zz = across(z, k)
        for i in range(2):
            arrived(got_full.at[i, zz], sum_send.at[0], sum_full.at[i, zz], at(z, y_up))
        view = unit(part, y, zz)
        added = view[...].astype(F32) + got_full[0, zz].astype(F32) + got_full[1, zz].astype(F32)
        if k == 0:
            total[...] = added
        else:
            view[...] = added.astype(BF16)
            out.send(view, got_z.at[k - 1], sum_send.at[15 + k], sum_z.at[k - 1], at(zz, y))
    for k in (1, 2, 3):
        arrived(got_z.at[k - 1], sum_send.at[0], sum_z.at[k - 1], at(across(z, k), y))
    result = total[...] + got_z[0].astype(F32) + got_z[1].astype(F32) + got_z[2].astype(F32)
    share = share_col[:, 0:1]
    unit(errors, y, z)[...] = (share * (share * result - unit(slots, y, z)[...].astype(F32))).astype(BF16)

    back = Gather(errors, gather_send.at[1], gather_full.at[1], gather_half.at[1], out)
    back.run()
    back.finish()
    last = [
        pltpu.make_async_copy(errors.at[0], errors_out.at[:, 0:half], store_sem.at[3]),
        pltpu.make_async_copy(errors.at[1], errors_out.at[:, half : 2 * half], store_sem.at[4]),
    ]
    for store in last:
        store.start()
    out.drain()
    for store in stores + last:
        store.wait()


def expert(tokens, routes, weights, up, down):
    width = tokens.shape[1]
    units = up.shape[1]
    half = width // 2
    slot_count = SIDE * SIDE * CAP
    hidden_total = units * SIDE * SIDE
    vmem = pl.BlockSpec(memory_space=pltpu.VMEM)
    hbm = pl.BlockSpec(memory_space=pl.ANY)
    dma = pltpu.SemaphoreType.DMA
    return pl.pallas_call(
        partial(expert_kernel, width ** (-0.5), hidden_total ** (-0.5)),
        out_shape=(
            jax.ShapeDtypeStruct((slot_count, width), BF16),
            jax.ShapeDtypeStruct((slot_count, width), BF16),
            jax.ShapeDtypeStruct((slot_count, units), F32),
        ),
        in_specs=[vmem, vmem, vmem, hbm, hbm],
        out_specs=(hbm, hbm, hbm),
        scratch_shapes=[
            pltpu.VMEM((2, slot_count, half), BF16),
            pltpu.VMEM((2, slot_count, half), BF16),
            pltpu.VMEM((width, units), BF16),
            pltpu.VMEM((units, width), BF16),
            pltpu.VMEM((slot_count, units), F32),
            pltpu.VMEM((slot_count, units), BF16),
            pltpu.VMEM((2, slot_count, half), BF16),
            pltpu.VMEM((2, SIDE, PAIR, half // 2), BF16),
            pltpu.VMEM((2, SIDE, PAIR, half), BF16),
            pltpu.VMEM((SIDE - 1, PAIR, half), BF16),
            pltpu.VMEM((PAIR, half), F32),
            pltpu.VMEM((STAGE, half + LANES), BF16),
            pltpu.VMEM((STAGE, half + LANES), BF16),
            pltpu.VMEM((PAIR, LANES), F32),
            dma((2,)),
            dma((5,)),
            dma((2,)),
            dma((2, 19)),
            dma((2, SIDE * SIDE)),
            dma((2, 2, SIDE * SIDE)),
            dma((19,)),
            dma((2, SIDE)),
            dma((2, SIDE)),
            dma((SIDE - 1,)),
        ],
        compiler_params=pltpu.CompilerParams(
            collective_id=0, has_side_effects=True, vmem_limit_bytes=48 * 1024 * 1024
        ),
        cost_estimate=pl.CostEstimate(
            flops=4 * slot_count * width * units, bytes_accessed=200_000_000, transcendentals=slot_count * units
        ),
    )(tokens, routes, weights, up, down)


def on_device(tokens, routing, router_weight, w_up, w_down, step_number):
    up, down = w_up[0], w_down[0]
    width, units = up.shape
    scale_up = width ** (-0.5)
    scale_down = (units * lax.axis_size("fsdp")) ** (-0.5)
    slots, errors, pre_act = expert(
        tokens[0], routing[0].T, router_weight[0].T.astype(F32), up, down
    )
    hidden = jax.nn.silu(pre_act).astype(BF16)
    grad_down = scale_down * lax.dot_general(
        hidden, errors, (((0,), (0,)), ((), ())), preferred_element_type=F32
    )
    moved_down = (down.astype(F32) - learn_rate * grad_down).astype(BF16)
    grad_hidden = scale_down * lax.dot_general(
        errors, down, (((1,), (1,)), ((), ())), preferred_element_type=F32
    )
    grad_pre = (grad_hidden * silu_slope(pre_act)).astype(BF16)
    grad_up = scale_up * lax.dot_general(
        slots, grad_pre, (((0,), (0,)), ((), ())), preferred_element_type=F32
    )
    moved_up = (up.astype(F32) - learn_rate * grad_up).astype(BF16)

    def swap(bit, moved):
        size = lax.axis_size("island")
        pairs = [(source, source ^ (1 << bit)) for source in range(size)]
        other = [lax.ppermute(value, "island", pairs) for value in moved]
        return tuple((0.5 * (a.astype(F32) + b.astype(F32))).astype(BF16) for a, b in zip(moved, other))

    levels = lax.axis_size("island").bit_length() - 1
    bit_index = jnp.remainder(step_number[0], jnp.int32(levels))
    new_up, new_down = lax.switch(
        bit_index, [partial(swap, bit) for bit in range(levels)], (moved_up, moved_down)
    )
    return (new_up[None], new_down[None])


def solution(mesh):
    placed = (
        P("island", "fsdp", None),
        P("island", "fsdp", None),
        P("island", "fsdp", None),
        P("island", None, "fsdp"),
        P("island", "fsdp", None),
        P(),
    )
    return jax.shard_map(
        on_device,
        mesh=mesh,
        in_specs=placed,
        out_specs=(P("island", None, "fsdp"), P("island", "fsdp", None)),
        check_vma=False,
    )
```

```python
from functools import partial

import jax
import jax.numpy as jnp
from jax import lax
from jax.experimental import pallas as pl
from jax.experimental.pallas import tpu as pltpu
from jax.sharding import PartitionSpec as P

MESH = pl.DeviceIdType.MESH
F32, BF16 = jnp.float32, jnp.bfloat16
CAP = 40
PAIR = 2 * CAP
STAGE = 48
SIDE = 4
GROUP = SIDE * PAIR
LANES = 128
TILE = 512
UNIT_TILE = 256

learn_rate = 4.0


def silu_slope(values):
    sig = jax.nn.sigmoid(values)
    return sig * (1.0 + values * (1.0 - sig))


def unit(ref, yy, zz, low=0, size=None):
    start = pl.multiple_of(((yy // 2) * SIDE + zz) * PAIR, 16)
    size = ref.shape[-1] if size is None else size
    return ref.at[yy % 2, pl.ds(start, PAIR), pl.ds(low, size)]


def place():
    me = lax.axis_index("fsdp")
    return me // SIDE, me % SIDE


def across(z, k):
    return (z, z + 1 - 2 * (z % 2), (z + 2) % SIDE, SIDE - 1 - z)[k]


class Sender:
    def __init__(self):
        self.started = []

    def send(self, src, dst, send_sem, recv_sem, device):
        copy = pltpu.make_async_remote_copy(
            src_ref=src,
            dst_ref=dst,
            send_sem=send_sem,
            recv_sem=recv_sem,
            device_id=device,
            device_id_type=MESH,
        )
        copy.start()
        self.started.append(copy)

    def drain(self):
        for copy in self.started:
            copy.wait_send()
        self.started = []


def arrived(dst, sems, recv_sem, device):
    pltpu.make_async_remote_copy(
        src_ref=dst, dst_ref=dst, send_sem=sems, recv_sem=recv_sem, device_id=device, device_id_type=MESH
    ).wait_recv()


def at(zz, yy):
    return {"fsdp": zz * SIDE + yy}


class Gather:
    def __init__(self, buf, send_sem, full_sem, half_sem, out):
        self.buf, self.send_sem, self.full_sem, self.half_sem, self.out = buf, send_sem, full_sem, half_sem, out
        self.z, self.y = place()
        self.part = buf.shape[-1] // 2

    def wait_full(self, yy, zz):
        view = unit(self.buf, yy, zz)
        arrived(view, self.send_sem.at[0], self.full_sem.at[yy * SIDE + zz], at(self.z, (self.y + 1) % SIDE))

    def push(self, k):
        z, y = self.z, self.y
        zz = across(z, k)
        if k > 0:
            self.wait_full(y, zz)
        view = unit(self.buf, y, zz)
        for i, step in enumerate((1, SIDE - 1)):
            self.out.send(
                view, view, self.send_sem.at[3 + 2 * k + i], self.full_sem.at[y * SIDE + zz], at(z, (y + step) % SIDE)
            )

    def forward(self, k):
        z, y = self.z, self.y
        zz = across(z, k)
        for i, step in enumerate((1, SIDE - 1)):
            source = (y + SIDE - step) % SIDE
            self.wait_full(source, zz)
            view = unit(self.buf, source, zz, i * self.part, self.part)
            self.out.send(
                view,
                view,
                self.send_sem.at[11 + 2 * k + i],
                self.half_sem.at[i, source * SIDE + zz],
                at(z, (y + step) % SIDE),
            )

    def open(self):
        z, y = self.z, self.y
        own = unit(self.buf, y, z)
        for k in (1, 2, 3):
            self.out.send(own, own, self.send_sem.at[k - 1], self.full_sem.at[y * SIDE + z], at(across(z, k), y))
        self.push(0)

    def steps(self):
        made = []
        for k in range(1, SIDE):
            made += [partial(self.push, k), partial(self.forward, k - 1)]
        return made + [partial(self.forward, SIDE - 1)]

    def run(self):
        self.open()
        for step in self.steps():
            step()

    def finish(self):
        z, y = self.z, self.y
        far = (y + 2) % SIDE
        for k in range(SIDE):
            zz = across(z, k)
            for i in range(2):
                view = unit(self.buf, far, zz, i * self.part, self.part)
                arrived(view, self.send_sem.at[0], self.half_sem.at[i, far * SIDE + zz], at(z, (y + 1) % SIDE))


def swapped(index, bit):
    step = 1 << bit
    return index + step - 2 * step * ((index // step) % 2)


def expert_kernel(
    bit,
    raw,
    scale_up,
    scale_down,
    tokens,
    routes,
    weights,
    up_hbm,
    down_hbm,
    up_out,
    down_out,
    slots,
    errors,
    up,
    down,
    pre,
    hidden,
    part,
    got_half,
    got_full,
    got_z,
    total,
    stage_out,
    stage_in,
    share_col,
    slope_in,
    up_mate,
    down_mate,
    load_sem,
    store_sem,
    stage_sem,
    gather_send,
    gather_full,
    gather_half,
    sum_send,
    sum_half,
    sum_full,
    sum_z,
    mate_send,
    mate_got,
    hidden_t,
    *more,
):
    z, y = place()
    half = tokens.shape[1] // 2
    quarter = half // 2
    units = up.shape[1]
    tile = min(TILE, half // 3)
    early = half // tile // 3
    out = Sender()
    y_up, y_down, y_far = (y + 1) % SIDE, (y + SIDE - 1) % SIDE, (y + 2) % SIDE
    y_pair = y + 1 - 2 * (y % 2)
    mate = {"island": swapped(lax.axis_index("island"), bit)}

    loads = [
        pltpu.make_async_copy(up_hbm, up, load_sem.at[0]),
        pltpu.make_async_copy(down_hbm, down, load_sem.at[1]),
    ]
    for load in loads:
        load.start()
    barrier = pltpu.get_barrier_semaphore()
    peers = [at(across(z, k), y) for k in (1, 2, 3)] + [at(z, y_up), at(z, y_down), mate]
    for peer in peers:
        pl.semaphore_signal(barrier, inc=1, device_id=peer, device_id_type=MESH)

    target0 = routes[0:1, :] == 0
    target1 = routes[1:2, :] == 0
    chosen = (target0 | target1).astype(F32)
    share_row = jnp.where(target0, weights[0:1, :], 0.0) + jnp.where(target1, weights[1:2, :], 0.0)
    count = chosen.shape[1]
    earlier = lax.broadcasted_iota(jnp.int32, (count, count), 0) <= lax.broadcasted_iota(jnp.int32, (count, count), 1)
    ranks = jnp.dot(
        jnp.broadcast_to(chosen, (8, count)).astype(BF16), earlier.astype(BF16), preferred_element_type=F32
    )[0:1, :]
    slot_ids = lax.broadcasted_iota(jnp.int32, (STAGE, count), 0).astype(F32)
    takes = (slot_ids == ranks - 1.0) & (chosen > 0.0) & (slot_ids < float(CAP))
    table = jnp.where(takes, 1.0, 0.0).astype(BF16)
    own_share = jnp.sum(jnp.where(takes, share_row, 0.0), axis=1, keepdims=True)
    mine = y % 2
    own_rows = jnp.dot(
        table, tokens[:, pl.ds(pl.multiple_of(mine * half, LANES), half)], preferred_element_type=F32
    )
    stage_out[:, 0:half] = jnp.dot(
        table, tokens[:, pl.ds(pl.multiple_of((1 - mine) * half, LANES), half)], preferred_element_type=F32
    ).astype(BF16)
    stage_out[:, half:] = jnp.broadcast_to(own_share, (STAGE, LANES)).astype(BF16)
    pl.semaphore_wait(barrier, len(peers))
    out.send(stage_out, stage_in, stage_sem.at[0], stage_sem.at[1], at(z, y_pair))
    arrived(stage_in, stage_sem.at[0], stage_sem.at[1], at(z, y_pair))
    other_rows = stage_in[:, 0:half].astype(F32)
    other_share = stage_in[:, half:].astype(F32)[0:CAP, 0:1]
    first = mine == 0
    own_rows, own_share, other_rows = own_rows[0:CAP], own_share[0:CAP], other_rows[0:CAP]
    rows = jnp.concatenate(
        [jnp.where(first, own_rows, other_rows), jnp.where(first, other_rows, own_rows)], axis=0
    ).astype(BF16)
    unit(slots, y, z)[...] = rows
    share_col[...] = jnp.broadcast_to(
        jnp.concatenate(
            [jnp.where(first, own_share, other_share), jnp.where(first, other_share, own_share)], axis=0
        ),
        (PAIR, LANES),
    )

    def gather(buf, i):
        return Gather(buf, gather_send.at[i], gather_full.at[i], gather_half.at[i], out)

    def tiles(ref, mat, i):
        begin = pl.ds(pl.multiple_of(i * tile, LANES), tile)
        return ref.at[begin, :] if mat == 0 else ref.at[:, begin]

    def tile_copy(src, mat, i):
        return pltpu.make_async_remote_copy(
            src_ref=tiles(src, mat, i),
            dst_ref=tiles((up_mate, down_mate)[mat], mat, i),
            send_sem=mate_send.at[mat, i],
            recv_sem=mate_got.at[mat, i],
            device_id=mate,
            device_id_type=MESH,
        )

    def send_tile(src, mat, i):
        tile_copy(src, mat, i).start()

    def wait_tile(mat, i):
        tile_copy((up_mate, down_mate)[mat], mat, i).wait_recv()

    spread = gather(slots, 0)
    if raw:
        slots_mate, errors_mate, hidden_mate, pre_mate, unit_send, unit_got = more
        spread_mate, back_mate = gather(slots_mate, 2), gather(errors_mate, 3)
        own_unit = unit(slots, y, z)
        out.send(own_unit, unit(slots_mate, y, z), unit_send.at[0], unit_got.at[0], mate)
        for i in range(2 * half // tile):
            send_tile(up_hbm, 0, i)
        for i in range(early):
            send_tile(down_hbm, 1, i)
    spread.run()
    if raw:
        arrived(unit(slots_mate, y, z), unit_send.at[0], unit_got.at[0], mate)
        spread_mate.open()

    def group_rows(group):
        return pl.ds(pl.multiple_of(group * GROUP, 16), GROUP)

    def lanes(i, size):
        return pl.ds(pl.multiple_of(i * size, LANES), size)

    def contract(block, left, right, right_t, finish):
        def step(n, carry):
            cols = lanes(n, UNIT_TILE)
            if right_t:
                first, second = right[cols, 0:half], right[cols, half:]
                dims = (((1,), (1,)), ((), ()))
            else:
                first, second = right[0:half, cols], right[half:, cols]
                dims = (((1,), (0,)), ((), ()))
            finish(
                cols,
                lax.dot_general(left[0, block, :], first, dims, preferred_element_type=F32)
                + lax.dot_general(left[1, block, :], second, dims, preferred_element_type=F32),
            )
            return carry

        lax.fori_loop(0, units // UNIT_TILE, step, 0)

    def ahead(group, slots, up, pre, hidden):
        block = group_rows(group)

        def finish(cols, values):
            values = scale_up * values
            pre[block, cols] = values
            hidden[block, cols] = jax.nn.silu(values).astype(BF16)

        contract(block, slots, up, False, finish)

    def column(yy):
        block = group_rows(yy // 2)
        side = yy % 2

        def step(j, carry):
            part[side, block, lanes(j, tile)] = (
                scale_down
                * jnp.dot(
                    hidden[block, :],
                    down[:, lanes(side * (half // tile) + j, tile)],
                    preferred_element_type=F32,
                )
            ).astype(BF16)
            return carry

        lax.fori_loop(0, half // tile, step, 0)

    def to(side):
        return (y + SIDE - 1 + 2 * side) % SIDE

    def send_rest(side):
        for k in (3, 2, 1, 0):
            zz = across(z, k)
            low = pl.multiple_of((1 - side) * quarter, LANES)
            out.send(
                unit(part, to(side), zz, low, quarter),
                got_full.at[side, zz, :, pl.ds(low, quarter)],
                sum_send.at[16 + 2 * k + side],
                sum_full.at[side, zz, 1],
                at(z, to(side)),
            )

    def send_far():
        for k in (3, 2, 1, 0):
            zz = across(z, k)
            for side in range(2):
                out.send(
                    unit(part, y_far, zz, side * quarter, quarter),
                    got_half.at[side, zz],
                    sum_send.at[2 * k + side],
                    sum_half.at[side, zz],
                    at(z, to(side)),
                )

    def add_far(k):
        zz = across(z, k)
        for side in range(2):
            low = side * quarter
            arrived(got_half.at[side, zz], sum_send.at[0], sum_half.at[side, zz], at(z, to(side)))
            view = unit(part, to(side), zz, low, quarter)
            view[...] = (view[...].astype(F32) + got_half[side, zz].astype(F32)).astype(BF16)
            out.send(
                view,
                got_full.at[side, zz, :, pl.ds(low, quarter)],
                sum_send.at[8 + 2 * k + side],
                sum_full.at[side, zz, 0],
                at(z, to(side)),
            )

    def collect(k):
        zz = across(z, k)
        for side in range(2):
            for low, sem in ((side * quarter, 0), ((1 - side) * quarter, 1)):
                arrived(
                    got_full.at[side, zz, :, pl.ds(low, quarter)], sum_send.at[0], sum_full.at[side, zz, sem], at(z, y_up)
                )
        view = unit(part, y, zz)
        added = view[...].astype(F32) + got_full[0, zz].astype(F32) + got_full[1, zz].astype(F32)
        if k == 0:
            total[...] = added
        else:
            view[...] = added.astype(BF16)
            out.send(view, got_z.at[k - 1], sum_send.at[23 + k], sum_z.at[k - 1], at(zz, y))

    for load in loads:
        load.wait()
    pair_side = 1 - y % 2
    ahead(y // 2, slots, up, pre, hidden)
    column(y_pair)
    send_rest(pair_side)
    spread.finish()
    ahead(1 - y // 2, slots, up, pre, hidden)
    column(y_far)
    send_far()
    column(to(1 - pair_side))
    send_rest(1 - pair_side)
    column(y)
    aside = spread_mate.steps() if raw else []
    add_far(3)
    add_far(2)
    collect(3)
    add_far(1)
    collect(2)
    add_far(0)
    for step in aside[:2]:
        step()
    collect(1)
    for step in aside[2:4]:
        step()
    collect(0)
    for step in aside[4:]:
        step()
    for k in (1, 2, 3):
        arrived(got_z.at[k - 1], sum_send.at[0], sum_z.at[k - 1], at(across(z, k), y))
    result = total[...] + got_z[0].astype(F32) + got_z[1].astype(F32) + got_z[2].astype(F32)
    share = share_col[:, 0:1]
    unit(errors, y, z)[...] = (share * (share * result - unit(slots, y, z)[...].astype(F32))).astype(BF16)

    back = gather(errors, 1)
    if raw:
        own_unit = unit(errors, y, z)
        out.send(own_unit, unit(errors_mate, y, z), unit_send.at[1], unit_got.at[1], mate)
        for i in range(early, 2 * half // tile):
            send_tile(down_hbm, 1, i)
    back.run()

    def slopes(group, errors, down, pre, slope_in):
        block = group_rows(group)

        def finish(cols, values):
            slope_in[block, cols] = (scale_down * values * silu_slope(pre[block, cols])).astype(BF16)

        contract(block, errors, down, True, finish)

    def turn(hidden):
        def step(j, carry):
            rows = pl.ds(pl.multiple_of(j * LANES, 16), LANES)
            hidden_t[:, lanes(j, LANES)] = hidden[rows, :].T
            return carry

        lax.fori_loop(0, hidden.shape[0] // LANES, step, 0)

    over_slots = (((0,), (0,)), ((), ()))

    def moved(mat, i, slots, errors, up, down, slope_in):
        side, cols = i // (half // tile), lanes(i % (half // tile), tile)
        if mat == 0:
            change = scale_up * lax.dot_general(
                slots[side, :, cols], slope_in[...], over_slots, preferred_element_type=F32
            )
            old = tiles(up, 0, i)[...]
        else:
            change = scale_down * jnp.dot(hidden_t[...], errors[side, :, cols], preferred_element_type=F32)
            old = tiles(down, 1, i)[...]
        return (old.astype(F32) - learn_rate * change).astype(BF16)

    own = (slots, errors, up, down, slope_in)
    count = 2 * half // tile

    def every_tile(body, first=0, last=None):
        def step(i, carry):
            for mat in (1, 0):
                body(mat, i)
            return carry

        lax.fori_loop(first, count if last is None else last, step, 0)

    def own_tile(mat, i):
        tiles((up, down)[mat], mat, i)[...] = moved(mat, i, *own)

    def store_of(mat, i):
        ref = (up_mate, down_mate)[mat]
        return pltpu.make_async_copy(
            tiles(ref, mat, i), tiles((up_out, down_out)[mat], mat, i), store_sem.at[mat, i]
        )

    def blend(mat, i, theirs):
        mine = tiles((up, down)[mat], mat, i)[...]
        tiles((up_mate, down_mate)[mat], mat, i)[...] = (
            0.5 * (mine.astype(F32) + theirs.astype(F32))
        ).astype(BF16)
        store_of(mat, i).start()

    if raw:
        arrived(unit(errors_mate, y, z), unit_send.at[1], unit_got.at[1], mate)
        back_mate.open()
        steps = back_mate.steps()
        slopes(y // 2, errors, down, pre, slope_in)
        steps[0]()
        back.finish()
        slopes(1 - y // 2, errors, down, pre, slope_in)
        steps[1]()
        turn(hidden)
        for n in range(4):
            steps[2 + n]()
            every_tile(own_tile, n * count // 4, (n + 1) * count // 4)
        steps[6]()
        spread_mate.finish()

        def wait_up(i, carry):
            wait_tile(0, i)
            return carry

        def wait_down(i, carry):
            wait_tile(1, i)
            return carry

        lax.fori_loop(0, count, wait_up, 0)
        for group in range(2):
            ahead(group, slots_mate, up_mate, pre_mate, hidden_mate)
        turn(hidden_mate)
        lax.fori_loop(0, count, wait_down, 0)
        slopes(y // 2, errors_mate, down_mate, pre_mate, slope_in)
        back_mate.finish()
        slopes(1 - y // 2, errors_mate, down_mate, pre_mate, slope_in)
        theirs = (slots_mate, errors_mate, up_mate, down_mate, slope_in)
        every_tile(lambda mat, i: blend(mat, i, moved(mat, i, *theirs)))
    else:
        turn(hidden)
        slopes(y // 2, errors, down, pre, slope_in)
        back.finish()
        slopes(1 - y // 2, errors, down, pre, slope_in)

        def move_and_send(mat, i):
            own_tile(mat, i)
            send_tile((up, down)[mat], mat, i)

        def meet(mat, i):
            wait_tile(mat, i)
            blend(mat, i, tiles((up_mate, down_mate)[mat], mat, i)[...])

        every_tile(move_and_send)
        every_tile(meet)

    def settle(mat, i):
        tile_copy((up_hbm, down_hbm)[mat] if raw else (up, down)[mat], mat, i).wait_send()
        store_of(mat, i).wait()

    every_tile(settle)
    out.drain()


def expert(bit, raw, tokens, routes, weights, up, down):
    width = tokens.shape[1]
    units = up.shape[1]
    half = width // 2
    tiles = width // min(TILE, half // 3)
    slot_count = SIDE * SIDE * CAP
    hidden_total = units * SIDE * SIDE
    vmem = pl.BlockSpec(memory_space=pltpu.VMEM)
    hbm = pl.BlockSpec(memory_space=pl.ANY)
    dma = pltpu.SemaphoreType.DMA
    all_rows = pltpu.VMEM((2, slot_count, half), BF16)
    gathers = 4 if raw else 2
    more = []
    if raw:
        more = [
            all_rows,
            all_rows,
            pltpu.VMEM((slot_count, units), BF16),
            pltpu.VMEM((slot_count, units), F32),
            dma((2,)),
            dma((2,)),
        ]
    return pl.pallas_call(
        partial(expert_kernel, bit, raw, width ** (-0.5), hidden_total ** (-0.5)),
        out_shape=(
            jax.ShapeDtypeStruct((width, units), BF16),
            jax.ShapeDtypeStruct((units, width), BF16),
        ),
        in_specs=[vmem, vmem, vmem, hbm, hbm],
        out_specs=(hbm, hbm),
        scratch_shapes=[
            all_rows,
            all_rows,
            pltpu.VMEM((width, units), BF16),
            pltpu.VMEM((units, width), BF16),
            pltpu.VMEM((slot_count, units), F32),
            pltpu.VMEM((slot_count, units), BF16),
            all_rows,
            pltpu.VMEM((2, SIDE, PAIR, half // 2), BF16),
            pltpu.VMEM((2, SIDE, PAIR, half), BF16),
            pltpu.VMEM((SIDE - 1, PAIR, half), BF16),
            pltpu.VMEM((PAIR, half), F32),
            pltpu.VMEM((STAGE, half + LANES), BF16),
            pltpu.VMEM((STAGE, half + LANES), BF16),
            pltpu.VMEM((PAIR, LANES), F32),
            pltpu.VMEM((slot_count, units), BF16),
            pltpu.VMEM((width, units), BF16),
            pltpu.VMEM((units, width), BF16),
            dma((2,)),
            dma((2, tiles)),
            dma((2,)),
            dma((gathers, 19)),
            dma((gathers, SIDE * SIDE)),
            dma((gathers, 2, SIDE * SIDE)),
            dma((27,)),
            dma((2, SIDE)),
            dma((2, SIDE, 2)),
            dma((SIDE - 1,)),
            dma((2, tiles)),
            dma((2, tiles)),
            pltpu.VMEM((units, slot_count), BF16),
        ]
        + more,
        compiler_params=pltpu.CompilerParams(
            collective_id=bit, has_side_effects=True, vmem_limit_bytes=60 * 1024 * 1024
        ),
        cost_estimate=pl.CostEstimate(
            flops=10 * slot_count * width * units, bytes_accessed=200_000_000, transcendentals=2 * slot_count * units
        ),
    )(tokens, routes, weights, up, down)


RAW_BITS = (1, 2)


def on_device(tokens, routing, router_weight, w_up, w_down, step_number):
    levels = lax.axis_size("island").bit_length() - 1
    bit_index = jnp.remainder(step_number[0], jnp.int32(levels))
    new_up, new_down = lax.switch(
        bit_index,
        [partial(expert, bit, bit in RAW_BITS) for bit in range(levels)],
        tokens[0],
        routing[0].T,
        router_weight[0].T.astype(F32),
        w_up[0],
        w_down[0],
    )
    return (new_up[None], new_down[None])


def solution(mesh):
    placed = (
        P("island", "fsdp", None),
        P("island", "fsdp", None),
        P("island", "fsdp", None),
        P("island", None, "fsdp"),
        P("island", "fsdp", None),
        P(),
    )
    return jax.shard_map(
        on_device,
        mesh=mesh,
        in_specs=placed,
        out_specs=(P("island", None, "fsdp"), P("island", "fsdp", None)),
        check_vma=False,
    )
```

```python
from functools import partial

import jax
import jax.numpy as jnp
from jax import lax
from jax.experimental import pallas as pl
from jax.experimental.pallas import tpu as pltpu
from jax.sharding import PartitionSpec as P

MESH = pl.DeviceIdType.MESH
F32, BF16 = jnp.float32, jnp.bfloat16
CAP = 40
PAIR = 2 * CAP
STAGE = 48
SIDE = 4
GROUP = SIDE * PAIR
LANES = 128
TILE = 512
UNIT_TILE = 256

learn_rate = 4.0


def silu_slope(values):
    sig = jax.nn.sigmoid(values)
    return sig * (1.0 + values * (1.0 - sig))


def unit(ref, yy, zz, low=0, size=None):
    start = pl.multiple_of(((yy // 2) * SIDE + zz) * PAIR, 16)
    size = ref.shape[-1] if size is None else size
    return ref.at[yy % 2, pl.ds(start, PAIR), pl.ds(low, size)]


def place():
    me = lax.axis_index("fsdp")
    return me // SIDE, me % SIDE


def across(z, k):
    return (z, z + 1 - 2 * (z % 2), (z + 2) % SIDE, SIDE - 1 - z)[k]


class Sender:
    def __init__(self):
        self.started = []

    def send(self, src, dst, send_sem, recv_sem, device):
        copy = pltpu.make_async_remote_copy(
            src_ref=src,
            dst_ref=dst,
            send_sem=send_sem,
            recv_sem=recv_sem,
            device_id=device,
            device_id_type=MESH,
        )
        copy.start()
        self.started.append(copy)

    def drain(self):
        for copy in self.started:
            copy.wait_send()
        self.started = []


def arrived(dst, sems, recv_sem, device):
    pltpu.make_async_remote_copy(
        src_ref=dst, dst_ref=dst, send_sem=sems, recv_sem=recv_sem, device_id=device, device_id_type=MESH
    ).wait_recv()


def at(zz, yy):
    return {"fsdp": zz * SIDE + yy}


class Gather:
    def __init__(self, buf, send_sem, full_sem, half_sem, out):
        self.buf, self.send_sem, self.full_sem, self.half_sem, self.out = buf, send_sem, full_sem, half_sem, out
        self.z, self.y = place()
        self.width = buf.shape[-1]

    def wait_full(self, yy, zz):
        view = unit(self.buf, yy, zz)
        arrived(view, self.send_sem.at[0], self.full_sem.at[yy * SIDE + zz], at(self.z, (self.y + 1) % SIDE))

    def push(self, k):
        z, y = self.z, self.y
        zz = across(z, k)
        if k > 0:
            self.wait_full(y, zz)
        view = unit(self.buf, y, zz)
        for i, step in enumerate((1, SIDE - 1)):
            self.out.send(
                view, view, self.send_sem.at[3 + 2 * k + i], self.full_sem.at[y * SIDE + zz], at(z, (y + step) % SIDE)
            )

    def side(self, k, i):
        size = self.width // (2 if k == 0 else 3)
        return i * (self.width - size), size

    def middle(self, zz):
        return unit(self.buf, (self.y + 2) % SIDE, zz, self.width // 3, self.width // 3)

    def forward(self, k):
        z, y = self.z, self.y
        zz = across(z, k)
        for i, step in enumerate((1, SIDE - 1)):
            source = (y + SIDE - step) % SIDE
            self.wait_full(source, zz)
            view = unit(self.buf, source, zz, *self.side(k, i))
            self.out.send(
                view,
                view,
                self.send_sem.at[11 + 2 * k + i],
                self.half_sem.at[i, source * SIDE + zz],
                at(z, (y + step) % SIDE),
            )

    def open(self):
        z, y = self.z, self.y
        own = unit(self.buf, y, z)
        for k in (1, 2, 3):
            self.out.send(own, own, self.send_sem.at[k - 1], self.full_sem.at[y * SIDE + z], at(across(z, k), y))
        self.push(0)

    def steps(self):
        made = []
        for k in range(1, SIDE):
            made += [partial(self.push, k), partial(self.forward, k - 1)]
        return made + [self.share_far, partial(self.forward, SIDE - 1)]

    def run(self):
        self.open()
        for step in self.steps():
            step()

    def wait_far(self, k):
        z, y = self.z, self.y
        far, zz = (y + 2) % SIDE, across(z, k)
        for i in range(2):
            view = unit(self.buf, far, zz, *self.side(k, i))
            arrived(view, self.send_sem.at[0], self.half_sem.at[i, far * SIDE + zz], at(z, (y + 1) % SIDE))

    def share_far(self):
        z, y = self.z, self.y
        self.wait_far(0)
        view = self.middle(z)
        for k in (1, 2, 3):
            self.out.send(view, view, self.send_sem.at[18 + k], self.half_sem.at[2, z], at(across(z, k), y))

    def finish(self):
        for k in (1, 2, 3):
            self.wait_far(k)
        for k in (1, 2, 3):
            zz = across(self.z, k)
            arrived(self.middle(zz), self.send_sem.at[0], self.half_sem.at[2, zz], at(zz, self.y))


def swapped(index, bit):
    step = 1 << bit
    return index + step - 2 * step * ((index // step) % 2)


def expert_kernel(
    bit,
    raw,
    scale_up,
    scale_down,
    tokens,
    routes,
    weights,
    up_hbm,
    down_hbm,
    up_out,
    down_out,
    slots,
    errors,
    up,
    down,
    pre,
    hidden,
    part,
    got_half,
    got_full,
    got_z,
    total,
    stage_out,
    stage_in,
    share_col,
    slope_in,
    up_mate,
    down_mate,
    load_sem,
    store_sem,
    stage_sem,
    gather_send,
    gather_full,
    gather_half,
    sum_send,
    sum_half,
    sum_full,
    sum_z,
    mate_send,
    mate_got,
    hidden_t,
    slots_t,
    got_third,
    third_got,
    *more,
):
    z, y = place()
    half = tokens.shape[1] // 2
    units = up.shape[1]
    tile = min(TILE, half // 3)
    early = max(2 * half // tile // 3, 1)
    out = Sender()
    y_up, y_down, y_far = (y + 1) % SIDE, (y + SIDE - 1) % SIDE, (y + 2) % SIDE
    y_pair = y + 1 - 2 * (y % 2)
    mate = {"island": swapped(lax.axis_index("island"), bit)}

    def tiles(ref, mat, i):
        begin = pl.ds(pl.multiple_of(i * tile, LANES), tile)
        return ref.at[begin, :] if mat == 0 else ref.at[:, begin]

    def tile_copy(src, mat, i):
        return pltpu.make_async_remote_copy(
            src_ref=tiles(src, mat, i),
            dst_ref=tiles((up_mate, down_mate)[mat], mat, i),
            send_sem=mate_send.at[mat, i],
            recv_sem=mate_got.at[mat, i],
            device_id=mate,
            device_id_type=MESH,
        )

    def send_tile(src, mat, i):
        tile_copy(src, mat, i).start()

    def wait_tile(mat, i):
        tile_copy((up_mate, down_mate)[mat], mat, i).wait_recv()

    loads = [
        pltpu.make_async_copy(up_hbm, up, load_sem.at[0]),
        pltpu.make_async_copy(down_hbm, down, load_sem.at[1]),
    ]
    for load in loads:
        load.start()
    barrier = pltpu.get_barrier_semaphore()
    peers = [at(across(z, k), y) for k in (1, 2, 3)] + [at(z, y_up), at(z, y_down), mate]
    for peer in peers:
        pl.semaphore_signal(barrier, inc=1, device_id=peer, device_id_type=MESH)

    target0 = routes[0:1, :] == 0
    target1 = routes[1:2, :] == 0
    chosen = (target0 | target1).astype(F32)
    weight = weights[...].astype(F32)
    share_row = jnp.where(target0, weight[0:1, :], 0.0) + jnp.where(target1, weight[1:2, :], 0.0)
    count = chosen.shape[1]
    earlier = lax.broadcasted_iota(jnp.int32, (count, count), 0) <= lax.broadcasted_iota(jnp.int32, (count, count), 1)
    ranks = jnp.dot(
        jnp.broadcast_to(chosen, (8, count)).astype(BF16), earlier.astype(BF16), preferred_element_type=F32
    )[0:1, :]
    slot_ids = lax.broadcasted_iota(jnp.int32, (STAGE, count), 0).astype(F32)
    takes = (slot_ids == ranks - 1.0) & (chosen > 0.0) & (slot_ids < float(CAP))
    table = jnp.where(takes, 1.0, 0.0).astype(BF16)
    own_share = jnp.sum(jnp.where(takes, share_row, 0.0), axis=1, keepdims=True)
    mine = y % 2
    own_rows = jnp.dot(
        table, tokens[:, pl.ds(pl.multiple_of(mine * half, LANES), half)], preferred_element_type=F32
    )
    stage_out[:, 0:half] = jnp.dot(
        table, tokens[:, pl.ds(pl.multiple_of((1 - mine) * half, LANES), half)], preferred_element_type=F32
    ).astype(BF16)
    stage_out[:, half:] = jnp.broadcast_to(own_share, (STAGE, LANES)).astype(BF16)
    pl.semaphore_wait(barrier, len(peers))
    out.send(stage_out, stage_in, stage_sem.at[0], stage_sem.at[1], at(z, y_pair))
    if raw:
        for i in range(early):
            send_tile(up_hbm, 0, i)
    arrived(stage_in, stage_sem.at[0], stage_sem.at[1], at(z, y_pair))
    other_rows = stage_in[:, 0:half].astype(F32)
    other_share = stage_in[:, half:].astype(F32)[0:CAP, 0:1]
    first = mine == 0
    own_rows, own_share, other_rows = own_rows[0:CAP], own_share[0:CAP], other_rows[0:CAP]
    rows = jnp.concatenate(
        [jnp.where(first, own_rows, other_rows), jnp.where(first, other_rows, own_rows)], axis=0
    ).astype(BF16)
    unit(slots, y, z)[...] = rows
    share_col[...] = jnp.broadcast_to(
        jnp.concatenate(
            [jnp.where(first, own_share, other_share), jnp.where(first, other_share, own_share)], axis=0
        ),
        (PAIR, LANES),
    )

    def gather(buf, i):
        return Gather(buf, gather_send.at[i], gather_full.at[i], gather_half.at[i], out)

    spread = gather(slots, 0)
    if raw:
        slots_mate, errors_mate, hidden_mate, pre_mate, unit_send, unit_got = more
        spread_mate, back_mate = gather(slots_mate, 2), gather(errors_mate, 3)
        own_unit = unit(slots, y, z)
        out.send(own_unit, unit(slots_mate, y, z), unit_send.at[0], unit_got.at[0], mate)
        for i in range(early, 2 * half // tile):
            send_tile(up_hbm, 0, i)
        for i in range(early):
            send_tile(down_hbm, 1, i)
    spread.run()
    if raw:
        arrived(unit(slots_mate, y, z), unit_send.at[0], unit_got.at[0], mate)
        spread_mate.open()

    def group_rows(group):
        return pl.ds(pl.multiple_of(group * GROUP, 16), GROUP)

    def lanes(i, size):
        return pl.ds(pl.multiple_of(i * size, LANES), size)

    def contract(block, left, right, right_t, finish):
        def step(n, carry):
            cols = lanes(n, UNIT_TILE)
            if right_t:
                first, second = right[cols, 0:half], right[cols, half:]
                dims = (((1,), (1,)), ((), ()))
            else:
                first, second = right[0:half, cols], right[half:, cols]
                dims = (((1,), (0,)), ((), ()))
            finish(
                cols,
                lax.dot_general(left[0, block, :], first, dims, preferred_element_type=F32)
                + lax.dot_general(left[1, block, :], second, dims, preferred_element_type=F32),
            )
            return carry

        lax.fori_loop(0, units // UNIT_TILE, step, 0)

    def ahead(group, slots, up, pre, hidden):
        block = group_rows(group)

        def finish(cols, values):
            values = scale_up * values
            pre[block, cols] = values
            hidden[block, cols] = jax.nn.silu(values).astype(BF16)

        contract(block, slots, up, False, finish)

    def column(yy):
        block = group_rows(yy // 2)
        side = yy % 2

        def step(j, carry):
            part[side, block, lanes(j, tile)] = (
                scale_down
                * jnp.dot(
                    hidden[block, :],
                    down[:, lanes(side * (half // tile) + j, tile)],
                    preferred_element_type=F32,
                )
            ).astype(BF16)
            return carry

        lax.fori_loop(0, half // tile, step, 0)

    def to(side):
        return (y + SIDE - 1 + 2 * side) % SIDE

    def size_of(k):
        return half // (2 if k == 0 else 3)

    def far_cols(k, side):
        return side * (half - size_of(k)), size_of(k)

    def rest_cols(k, side):
        return pl.multiple_of((1 - side) * size_of(k), LANES), half - size_of(k)

    def send_rest(side):
        for k in (3, 2, 1, 0):
            zz = across(z, k)
            low, size = rest_cols(k, side)
            out.send(
                unit(part, to(side), zz, low, size),
                got_full.at[side, zz, :, pl.ds(low, size)],
                sum_send.at[16 + 2 * k + side],
                sum_full.at[side, zz, 1],
                at(z, to(side)),
            )

    def send_middle():
        for k in (1, 2, 3):
            out.send(
                unit(part, y_far, across(z, k), half // 3, half // 3),
                got_third.at[k - 1],
                sum_send.at[26 + k],
                third_got.at[k - 1],
                at(across(z, k), y),
            )

    def add_middle():
        for k in (1, 2, 3):
            arrived(got_third.at[k - 1], sum_send.at[0], third_got.at[k - 1], at(across(z, k), y))
        view = unit(part, y_far, z, half // 3, half // 3)
        view[...] = (
            view[...].astype(F32) + got_third[0].astype(F32) + got_third[1].astype(F32) + got_third[2].astype(F32)
        ).astype(BF16)

    def send_far(k):
        zz = across(z, k)
        for side in range(2):
            low, size = far_cols(k, side)
            out.send(
                unit(part, y_far, zz, low, size),
                got_half.at[side, zz, :, pl.ds(0, size)],
                sum_send.at[2 * k + side],
                sum_half.at[side, zz],
                at(z, to(side)),
            )

    def add_far(k):
        zz = across(z, k)
        for side in range(2):
            low, size = far_cols(k, side)
            got = got_half.at[side, zz, :, pl.ds(0, size)]
            arrived(got, sum_send.at[0], sum_half.at[side, zz], at(z, to(side)))
            view = unit(part, to(side), zz, low, size)
            view[...] = (view[...].astype(F32) + got[...].astype(F32)).astype(BF16)
            out.send(
                view,
                got_full.at[side, zz, :, pl.ds(low, size)],
                sum_send.at[8 + 2 * k + side],
                sum_full.at[side, zz, 0],
                at(z, to(side)),
            )

    def collect(k):
        zz = across(z, k)
        for side in range(2):
            for sem, (low, size) in enumerate((far_cols(k, side), rest_cols(k, side))):
                arrived(
                    got_full.at[side, zz, :, pl.ds(low, size)], sum_send.at[0], sum_full.at[side, zz, sem], at(z, y_up)
                )
        view = unit(part, y, zz)
        added = view[...].astype(F32) + got_full[0, zz].astype(F32) + got_full[1, zz].astype(F32)
        if k == 0:
            total[...] = added
        else:
            view[...] = added.astype(BF16)
            out.send(view, got_z.at[k - 1], sum_send.at[23 + k], sum_z.at[k - 1], at(zz, y))

    for load in loads:
        load.wait()
    pair_side = 1 - y % 2
    ahead(y // 2, slots, up, pre, hidden)
    column(y_pair)
    send_rest(pair_side)
    spread.finish()
    ahead(1 - y // 2, slots, up, pre, hidden)
    column(y_far)
    send_middle()
    for k in (3, 2, 1):
        send_far(k)
    column(to(1 - pair_side))
    send_rest(1 - pair_side)
    column(y)
    add_middle()
    send_far(0)
    aside = spread_mate.steps() if raw else []
    add_far(3)
    add_far(2)
    collect(3)
    add_far(1)
    collect(2)
    add_far(0)
    for step in aside[:2]:
        step()
    collect(1)
    for step in aside[2:4]:
        step()
    collect(0)
    for step in aside[4:]:
        step()
    for k in (1, 2, 3):
        arrived(got_z.at[k - 1], sum_send.at[0], sum_z.at[k - 1], at(across(z, k), y))
    result = total[...] + got_z[0].astype(F32) + got_z[1].astype(F32) + got_z[2].astype(F32)
    share = share_col[:, 0:1]
    unit(errors, y, z)[...] = (share * (share * result - unit(slots, y, z)[...].astype(F32))).astype(BF16)

    back = gather(errors, 1)
    if raw:
        own_unit = unit(errors, y, z)
        out.send(own_unit, unit(errors_mate, y, z), unit_send.at[1], unit_got.at[1], mate)
        for i in range(early, 2 * half // tile):
            send_tile(down_hbm, 1, i)
    back.run()

    def slopes(group, errors, down, pre, slope_in):
        block = group_rows(group)

        def finish(cols, values):
            slope_in[block, cols] = (scale_down * values * silu_slope(pre[block, cols])).astype(BF16)

        contract(block, errors, down, True, finish)

    def both(body):
        def step(group, carry):
            body(group)
            return carry

        lax.fori_loop(0, 2, step, 0)

    def turn(hidden, slots):
        def step(j, carry):
            rows = pl.ds(pl.multiple_of(j * LANES, 16), LANES)
            hidden_t[rows, :] = hidden[:, lanes(j, LANES)].T
            return carry

        def step_slots(j, carry):
            blocks = half // LANES
            rows = pl.ds(pl.multiple_of(j * LANES, 16), LANES)
            slots_t[rows, :] = slots[j // blocks, :, lanes(j % blocks, LANES)].T
            return carry

        lax.fori_loop(0, units // LANES, step, 0)
        lax.fori_loop(0, 2 * half // LANES, step_slots, 0)

    def moved(mat, i, errors, up, down, slope_in):
        if mat == 0:
            rows = pl.ds(pl.multiple_of(i * tile, LANES), tile)
            change = scale_up * jnp.dot(slots_t[rows, :], slope_in[...], preferred_element_type=F32)
            old = tiles(up, 0, i)[...]
        else:
            side, cols = i // (half // tile), lanes(i % (half // tile), tile)
            change = scale_down * jnp.dot(hidden_t[...], errors[side, :, cols], preferred_element_type=F32)
            old = tiles(down, 1, i)[...]
        return (old.astype(F32) - learn_rate * change).astype(BF16)

    own = (errors, up, down, slope_in)
    count = 2 * half // tile

    def every_tile(body, first=0, last=None):
        def step(i, carry):
            for mat in (1, 0):
                body(mat, i)
            return carry

        lax.fori_loop(first, count if last is None else last, step, 0)

    def own_tile(mat, i):
        tiles((up, down)[mat], mat, i)[...] = moved(mat, i, *own)

    def store_of(mat, i):
        ref = (up_mate, down_mate)[mat]
        return pltpu.make_async_copy(
            tiles(ref, mat, i), tiles((up_out, down_out)[mat], mat, i), store_sem.at[mat, i]
        )

    def blend(mat, i, theirs):
        mine = tiles((up, down)[mat], mat, i)[...]
        tiles((up_mate, down_mate)[mat], mat, i)[...] = (
            0.5 * (mine.astype(F32) + theirs.astype(F32))
        ).astype(BF16)
        store_of(mat, i).start()

    if raw:
        arrived(unit(errors_mate, y, z), unit_send.at[1], unit_got.at[1], mate)
        back_mate.open()
        steps = back_mate.steps()
        spread_mate.finish()

        def wait_up(i, carry):
            wait_tile(0, i)
            return carry

        def wait_down(i, carry):
            wait_tile(1, i)
            return carry

        lax.fori_loop(0, count, wait_up, 0)
        for step in steps[:1]:
            step()
        both(lambda group: ahead(group, slots_mate, up_mate, pre_mate, hidden_mate))
        for step in steps[1:3]:
            step()
        back.finish()
        both(lambda group: slopes(group, errors, down, pre, slope_in))
        for step in steps[3:5]:
            step()
        turn(hidden, slots)
        every_tile(own_tile)
        for step in steps[5:]:
            step()
        turn(hidden_mate, slots_mate)
        lax.fori_loop(0, count, wait_down, 0)
        back_mate.finish()
        both(lambda group: slopes(group, errors_mate, down_mate, pre_mate, slope_in))
        theirs = (errors_mate, up_mate, down_mate, slope_in)
        every_tile(lambda mat, i: blend(mat, i, moved(mat, i, *theirs)))
    else:
        turn(hidden, slots)
        back.finish()
        both(lambda group: slopes(group, errors, down, pre, slope_in))

        def move_and_send(mat, i):
            own_tile(mat, i)
            send_tile((up, down)[mat], mat, i)

        def meet(mat, i):
            wait_tile(mat, i)
            blend(mat, i, tiles((up_mate, down_mate)[mat], mat, i)[...])

        every_tile(move_and_send)
        every_tile(meet)

    def settle(mat, i):
        tile_copy((up_hbm, down_hbm)[mat] if raw else (up, down)[mat], mat, i).wait_send()
        store_of(mat, i).wait()

    every_tile(settle)
    out.drain()


def expert(bit, raw, tokens, routes, weights, up, down):
    width = tokens.shape[1]
    units = up.shape[1]
    half = width // 2
    tiles = width // min(TILE, half // 3)
    slot_count = SIDE * SIDE * CAP
    hidden_total = units * SIDE * SIDE
    vmem = pl.BlockSpec(memory_space=pltpu.VMEM)
    hbm = pl.BlockSpec(memory_space=pl.ANY)
    dma = pltpu.SemaphoreType.DMA
    all_rows = pltpu.VMEM((2, slot_count, half), BF16)
    gathers = 4 if raw else 2
    more = []
    if raw:
        more = [
            all_rows,
            all_rows,
            pltpu.VMEM((slot_count, units), BF16),
            pltpu.VMEM((slot_count, units), F32),
            dma((2,)),
            dma((2,)),
        ]
    return pl.pallas_call(
        partial(expert_kernel, bit, raw, width ** (-0.5), hidden_total ** (-0.5)),
        out_shape=(
            jax.ShapeDtypeStruct((width, units), BF16),
            jax.ShapeDtypeStruct((units, width), BF16),
        ),
        in_specs=[vmem, vmem, vmem, hbm, hbm],
        out_specs=(hbm, hbm),
        scratch_shapes=[
            all_rows,
            all_rows,
            pltpu.VMEM((width, units), BF16),
            pltpu.VMEM((units, width), BF16),
            pltpu.VMEM((slot_count, units), F32),
            pltpu.VMEM((slot_count, units), BF16),
            all_rows,
            pltpu.VMEM((2, SIDE, PAIR, half // 2), BF16),
            pltpu.VMEM((2, SIDE, PAIR, half), BF16),
            pltpu.VMEM((SIDE - 1, PAIR, half), BF16),
            pltpu.VMEM((PAIR, half), F32),
            pltpu.VMEM((STAGE, half + LANES), BF16),
            pltpu.VMEM((STAGE, half + LANES), BF16),
            pltpu.VMEM((PAIR, LANES), F32),
            pltpu.VMEM((slot_count, units), BF16),
            pltpu.VMEM((width, units), BF16),
            pltpu.VMEM((units, width), BF16),
            dma((2,)),
            dma((2, tiles)),
            dma((2,)),
            dma((gathers, 22)),
            dma((gathers, SIDE * SIDE)),
            dma((gathers, 3, SIDE * SIDE)),
            dma((30,)),
            dma((2, SIDE)),
            dma((2, SIDE, 2)),
            dma((SIDE - 1,)),
            dma((2, tiles)),
            dma((2, tiles)),
            pltpu.VMEM((units, slot_count), BF16),
            pltpu.VMEM((width, slot_count), BF16),
            pltpu.VMEM((SIDE - 1, PAIR, half // 3), BF16),
            dma((SIDE - 1,)),
        ]
        + more,
        compiler_params=pltpu.CompilerParams(
            collective_id=bit, has_side_effects=True, vmem_limit_bytes=56 * 1024 * 1024
        ),
        cost_estimate=pl.CostEstimate(
            flops=10 * slot_count * width * units, bytes_accessed=200_000_000, transcendentals=2 * slot_count * units
        ),
    )(tokens, routes, weights, up, down)


RAW_BITS = (1, 2)


def on_device(tokens, routing, router_weight, w_up, w_down, step_number):
    levels = lax.axis_size("island").bit_length() - 1
    bit_index = jnp.remainder(step_number[0], jnp.int32(levels))
    new_up, new_down = lax.switch(
        bit_index,
        [partial(expert, bit, bit in RAW_BITS) for bit in range(levels)],
        tokens[0],
        routing[0].T,
        router_weight[0].T,
        w_up[0],
        w_down[0],
    )
    return (new_up[None], new_down[None])


def solution(mesh):
    placed = (
        P("island", "fsdp", None),
        P("island", "fsdp", None),
        P("island", "fsdp", None),
        P("island", None, "fsdp"),
        P("island", "fsdp", None),
        P(),
    )
    return jax.shard_map(
        on_device,
        mesh=mesh,
        in_specs=placed,
        out_specs=(P("island", None, "fsdp"), P("island", "fsdp", None)),
        check_vma=False,
    )
```

```python
from functools import partial

import jax
import jax.numpy as jnp
from jax import lax
from jax.experimental import pallas as pl
from jax.experimental.pallas import tpu as pltpu
from jax.sharding import PartitionSpec as P

MESH = pl.DeviceIdType.MESH
F32, BF16 = jnp.float32, jnp.bfloat16
CAP = 40
PAIR = 2 * CAP
STAGE = 48
SIDE = 4
GROUP = SIDE * PAIR
LANES = 128
TILE = 512
UNIT_TILE = 256

learn_rate = 4.0


def silu_slope(values):
    sig = jax.nn.sigmoid(values)
    return sig * (1.0 + values * (1.0 - sig))


def unit(ref, yy, zz, low=0, size=None):
    start = pl.multiple_of(((yy // 2) * SIDE + zz) * PAIR, 16)
    size = ref.shape[-1] if size is None else size
    return ref.at[yy % 2, pl.ds(start, PAIR), pl.ds(low, size)]


def place():
    me = lax.axis_index("fsdp")
    return me // SIDE, me % SIDE


def across(z, k):
    return (z, z + 1 - 2 * (z % 2), (z + 2) % SIDE, SIDE - 1 - z)[k]


class Sender:
    def __init__(self):
        self.started = []

    def send(self, src, dst, send_sem, recv_sem, device):
        copy = pltpu.make_async_remote_copy(
            src_ref=src,
            dst_ref=dst,
            send_sem=send_sem,
            recv_sem=recv_sem,
            device_id=device,
            device_id_type=MESH,
        )
        copy.start()
        self.started.append(copy)

    def drain(self):
        for copy in self.started:
            copy.wait_send()
        self.started = []


def arrived(dst, sems, recv_sem, device):
    pltpu.make_async_remote_copy(
        src_ref=dst, dst_ref=dst, send_sem=sems, recv_sem=recv_sem, device_id=device, device_id_type=MESH
    ).wait_recv()


def at(zz, yy):
    return {"fsdp": zz * SIDE + yy}


class Gather:
    def __init__(self, buf, send_sem, full_sem, half_sem, out):
        self.buf, self.send_sem, self.full_sem, self.half_sem, self.out = buf, send_sem, full_sem, half_sem, out
        self.z, self.y = place()
        self.width = buf.shape[-1]

    def wait_full(self, yy, zz):
        view = unit(self.buf, yy, zz)
        arrived(view, self.send_sem.at[0], self.full_sem.at[yy * SIDE + zz], at(self.z, (self.y + 1) % SIDE))

    def push(self, k):
        z, y = self.z, self.y
        zz = across(z, k)
        if k > 0:
            self.wait_full(y, zz)
        view = unit(self.buf, y, zz)
        for i, step in enumerate((1, SIDE - 1)):
            self.out.send(
                view, view, self.send_sem.at[3 + 2 * k + i], self.full_sem.at[y * SIDE + zz], at(z, (y + step) % SIDE)
            )

    def side(self, k, i):
        size = self.width // (2 if k == 0 else 3)
        return i * (self.width - size), size

    def middle(self, zz):
        return unit(self.buf, (self.y + 2) % SIDE, zz, self.width // 3, self.width // 3)

    def forward(self, k):
        z, y = self.z, self.y
        zz = across(z, k)
        for i, step in enumerate((1, SIDE - 1)):
            source = (y + SIDE - step) % SIDE
            self.wait_full(source, zz)
            view = unit(self.buf, source, zz, *self.side(k, i))
            self.out.send(
                view,
                view,
                self.send_sem.at[11 + 2 * k + i],
                self.half_sem.at[i, source * SIDE + zz],
                at(z, (y + step) % SIDE),
            )

    def open(self):
        z, y = self.z, self.y
        own = unit(self.buf, y, z)
        for k in (1, 2, 3):
            self.out.send(own, own, self.send_sem.at[k - 1], self.full_sem.at[y * SIDE + z], at(across(z, k), y))
        self.push(0)

    def steps(self):
        made = []
        for k in range(1, SIDE):
            made += [partial(self.push, k), partial(self.forward, k - 1)]
        return made + [self.share_far, partial(self.forward, SIDE - 1)]

    def run(self):
        self.open()
        for step in self.steps():
            step()

    def wait_far(self, k):
        z, y = self.z, self.y
        far, zz = (y + 2) % SIDE, across(z, k)
        for i in range(2):
            view = unit(self.buf, far, zz, *self.side(k, i))
            arrived(view, self.send_sem.at[0], self.half_sem.at[i, far * SIDE + zz], at(z, (y + 1) % SIDE))

    def share_far(self):
        z, y = self.z, self.y
        self.wait_far(0)
        view = self.middle(z)
        for k in (1, 2, 3):
            self.out.send(view, view, self.send_sem.at[18 + k], self.half_sem.at[2, z], at(across(z, k), y))

    def finish(self):
        for k in (1, 2, 3):
            self.wait_far(k)
        for k in (1, 2, 3):
            zz = across(self.z, k)
            arrived(self.middle(zz), self.send_sem.at[0], self.half_sem.at[2, zz], at(zz, self.y))


def swapped(index, bit):
    step = 1 << bit
    return index + step - 2 * step * ((index // step) % 2)


def expert_kernel(
    bit,
    raw,
    scale_up,
    scale_down,
    tokens,
    routes,
    weights,
    up_hbm,
    down_hbm,
    up_out,
    down_out,
    slots,
    errors,
    up,
    down,
    pre,
    hidden,
    part,
    got_half,
    got_full,
    got_z,
    total,
    stage_out,
    stage_in,
    share_col,
    slope_in,
    up_mate,
    down_mate,
    load_sem,
    store_sem,
    stage_sem,
    gather_send,
    gather_full,
    gather_half,
    sum_send,
    sum_half,
    sum_full,
    sum_z,
    mate_send,
    mate_got,
    hidden_t,
    slots_t,
    got_third,
    third_got,
    *more,
):
    z, y = place()
    half = tokens.shape[1] // 2
    units = up.shape[1]
    tile = min(TILE, half // 3)
    early = max(2 * half // tile // 3, 1)
    out = Sender()
    y_up, y_down, y_far = (y + 1) % SIDE, (y + SIDE - 1) % SIDE, (y + 2) % SIDE
    y_pair = y + 1 - 2 * (y % 2)
    mate = {"island": swapped(lax.axis_index("island"), bit)}

    def tiles(ref, mat, i):
        begin = pl.ds(pl.multiple_of(i * tile, LANES), tile)
        return ref.at[begin, :] if mat == 0 else ref.at[:, begin]

    def tile_copy(src, mat, i):
        return pltpu.make_async_remote_copy(
            src_ref=tiles(src, mat, i),
            dst_ref=tiles((up_mate, down_mate)[mat], mat, i),
            send_sem=mate_send.at[mat, i],
            recv_sem=mate_got.at[mat, i],
            device_id=mate,
            device_id_type=MESH,
        )

    def send_tile(src, mat, i):
        tile_copy(src, mat, i).start()

    def wait_tile(mat, i):
        tile_copy((up_mate, down_mate)[mat], mat, i).wait_recv()

    loads = [
        pltpu.make_async_copy(up_hbm, up, load_sem.at[0]),
        pltpu.make_async_copy(down_hbm, down, load_sem.at[1]),
    ]
    for load in loads:
        load.start()
    barrier = pltpu.get_barrier_semaphore()
    peers = [at(across(z, k), y) for k in (1, 2, 3)] + [at(z, y_up), at(z, y_down), mate]
    for peer in peers:
        pl.semaphore_signal(barrier, inc=1, device_id=peer, device_id_type=MESH)

    target0 = routes[0:1, :] == 0
    target1 = routes[1:2, :] == 0
    chosen = (target0 | target1).astype(F32)
    weight = weights[...].astype(F32)
    share_row = jnp.where(target0, weight[0:1, :], 0.0) + jnp.where(target1, weight[1:2, :], 0.0)
    count = chosen.shape[1]
    earlier = lax.broadcasted_iota(jnp.int32, (count, count), 0) <= lax.broadcasted_iota(jnp.int32, (count, count), 1)
    ranks = jnp.dot(
        jnp.broadcast_to(chosen, (8, count)).astype(BF16), earlier.astype(BF16), preferred_element_type=F32
    )[0:1, :]
    slot_ids = lax.broadcasted_iota(jnp.int32, (STAGE, count), 0).astype(F32)
    takes = (slot_ids == ranks - 1.0) & (chosen > 0.0) & (slot_ids < float(CAP))
    table = jnp.where(takes, 1.0, 0.0).astype(BF16)
    own_share = jnp.sum(jnp.where(takes, share_row, 0.0), axis=1, keepdims=True)
    mine = y % 2
    own_rows = jnp.dot(
        table, tokens[:, pl.ds(pl.multiple_of(mine * half, LANES), half)], preferred_element_type=F32
    )
    stage_out[:, 0:half] = jnp.dot(
        table, tokens[:, pl.ds(pl.multiple_of((1 - mine) * half, LANES), half)], preferred_element_type=F32
    ).astype(BF16)
    stage_out[:, half:] = jnp.broadcast_to(own_share, (STAGE, LANES)).astype(BF16)
    pl.semaphore_wait(barrier, len(peers))
    out.send(stage_out, stage_in, stage_sem.at[0], stage_sem.at[1], at(z, y_pair))
    if raw:
        for i in range(early):
            send_tile(up_hbm, 0, i)
    arrived(stage_in, stage_sem.at[0], stage_sem.at[1], at(z, y_pair))
    other_rows = stage_in[:, 0:half].astype(F32)
    other_share = stage_in[:, half:].astype(F32)[0:CAP, 0:1]
    first = mine == 0
    own_rows, own_share, other_rows = own_rows[0:CAP], own_share[0:CAP], other_rows[0:CAP]
    rows = jnp.concatenate(
        [jnp.where(first, own_rows, other_rows), jnp.where(first, other_rows, own_rows)], axis=0
    ).astype(BF16)
    unit(slots, y, z)[...] = rows
    share_col[...] = jnp.broadcast_to(
        jnp.concatenate(
            [jnp.where(first, own_share, other_share), jnp.where(first, other_share, own_share)], axis=0
        ),
        (PAIR, LANES),
    )

    def gather(buf, i):
        return Gather(buf, gather_send.at[i], gather_full.at[i], gather_half.at[i], out)

    spread = gather(slots, 0)
    if raw:
        slots_mate, errors_mate, hidden_mate, pre_mate, unit_send, unit_got = more
        spread_mate, back_mate = gather(slots_mate, 2), gather(errors_mate, 3)
        own_unit = unit(slots, y, z)
        out.send(own_unit, unit(slots_mate, y, z), unit_send.at[0], unit_got.at[0], mate)
        for i in range(early, 2 * half // tile):
            send_tile(up_hbm, 0, i)
        for i in range(early):
            send_tile(down_hbm, 1, i)
    spread.run()
    if raw:
        arrived(unit(slots_mate, y, z), unit_send.at[0], unit_got.at[0], mate)
        spread_mate.open()

    def group_rows(group):
        return pl.ds(pl.multiple_of(group * GROUP, 16), GROUP)

    def lanes(i, size):
        return pl.ds(pl.multiple_of(i * size, LANES), size)

    def contract(block, left, right, right_t, finish):
        def step(n, carry):
            cols = lanes(n, UNIT_TILE)
            if right_t:
                first, second = right[cols, 0:half], right[cols, half:]
                dims = (((1,), (1,)), ((), ()))
            else:
                first, second = right[0:half, cols], right[half:, cols]
                dims = (((1,), (0,)), ((), ()))
            finish(
                cols,
                lax.dot_general(left[0, block, :], first, dims, preferred_element_type=F32)
                + lax.dot_general(left[1, block, :], second, dims, preferred_element_type=F32),
            )
            return carry

        lax.fori_loop(0, units // UNIT_TILE, step, 0)

    every = slice(None)

    def ahead(group, slots, up, pre, hidden):
        block = every if group is None else group_rows(group)

        def finish(cols, values):
            values = scale_up * values
            pre[block, cols] = values
            hidden[block, cols] = jax.nn.silu(values).astype(BF16)

        contract(block, slots, up, False, finish)

    def column(yy):
        block = group_rows(yy // 2)
        side = yy % 2

        def step(j, carry):
            part[side, block, lanes(j, tile)] = (
                scale_down
                * jnp.dot(
                    hidden[block, :],
                    down[:, lanes(side * (half // tile) + j, tile)],
                    preferred_element_type=F32,
                )
            ).astype(BF16)
            return carry

        lax.fori_loop(0, half // tile, step, 0)

    def to(side):
        return (y + SIDE - 1 + 2 * side) % SIDE

    def size_of(k):
        return half // (2 if k == 0 else 3)

    def far_cols(k, side):
        return side * (half - size_of(k)), size_of(k)

    def rest_cols(k, side):
        return pl.multiple_of((1 - side) * size_of(k), LANES), half - size_of(k)

    def send_rest(side):
        for k in (3, 2, 1, 0):
            zz = across(z, k)
            low, size = rest_cols(k, side)
            out.send(
                unit(part, to(side), zz, low, size),
                got_full.at[side, zz, :, pl.ds(low, size)],
                sum_send.at[16 + 2 * k + side],
                sum_full.at[side, zz, 1],
                at(z, to(side)),
            )

    def send_middle():
        for k in (1, 2, 3):
            out.send(
                unit(part, y_far, across(z, k), half // 3, half // 3),
                got_third.at[k - 1],
                sum_send.at[26 + k],
                third_got.at[k - 1],
                at(across(z, k), y),
            )

    def add_middle():
        for k in (1, 2, 3):
            arrived(got_third.at[k - 1], sum_send.at[0], third_got.at[k - 1], at(across(z, k), y))
        view = unit(part, y_far, z, half // 3, half // 3)
        view[...] = (
            view[...].astype(F32) + got_third[0].astype(F32) + got_third[1].astype(F32) + got_third[2].astype(F32)
        ).astype(BF16)

    def send_far(k):
        zz = across(z, k)
        for side in range(2):
            low, size = far_cols(k, side)
            out.send(
                unit(part, y_far, zz, low, size),
                got_half.at[side, zz, :, pl.ds(0, size)],
                sum_send.at[2 * k + side],
                sum_half.at[side, zz],
                at(z, to(side)),
            )

    def add_far(k):
        zz = across(z, k)
        for side in range(2):
            low, size = far_cols(k, side)
            got = got_half.at[side, zz, :, pl.ds(0, size)]
            arrived(got, sum_send.at[0], sum_half.at[side, zz], at(z, to(side)))
            view = unit(part, to(side), zz, low, size)
            view[...] = (view[...].astype(F32) + got[...].astype(F32)).astype(BF16)
            out.send(
                view,
                got_full.at[side, zz, :, pl.ds(low, size)],
                sum_send.at[8 + 2 * k + side],
                sum_full.at[side, zz, 0],
                at(z, to(side)),
            )

    def collect(k):
        zz = across(z, k)
        for side in range(2):
            for sem, (low, size) in enumerate((far_cols(k, side), rest_cols(k, side))):
                arrived(
                    got_full.at[side, zz, :, pl.ds(low, size)], sum_send.at[0], sum_full.at[side, zz, sem], at(z, y_up)
                )
        view = unit(part, y, zz)
        added = view[...].astype(F32) + got_full[0, zz].astype(F32) + got_full[1, zz].astype(F32)
        if k == 0:
            total[...] = added
        else:
            view[...] = added.astype(BF16)
            out.send(view, got_z.at[k - 1], sum_send.at[23 + k], sum_z.at[k - 1], at(zz, y))

    for load in loads:
        load.wait()
    pair_side = 1 - y % 2
    ahead(y // 2, slots, up, pre, hidden)
    column(y_pair)
    send_rest(pair_side)
    spread.finish()
    ahead(1 - y // 2, slots, up, pre, hidden)
    column(y_far)
    send_middle()
    for k in (3, 2, 1):
        send_far(k)
    column(to(1 - pair_side))
    send_rest(1 - pair_side)
    column(y)
    add_middle()
    send_far(0)
    aside = spread_mate.steps() if raw else []
    add_far(3)
    add_far(2)
    collect(3)
    add_far(1)
    collect(2)
    add_far(0)
    for step in aside[:2]:
        step()
    collect(1)
    for step in aside[2:4]:
        step()
    collect(0)
    for step in aside[4:]:
        step()
    for k in (1, 2, 3):
        arrived(got_z.at[k - 1], sum_send.at[0], sum_z.at[k - 1], at(across(z, k), y))
    result = total[...] + got_z[0].astype(F32) + got_z[1].astype(F32) + got_z[2].astype(F32)
    share = share_col[:, 0:1]
    unit(errors, y, z)[...] = (share * (share * result - unit(slots, y, z)[...].astype(F32))).astype(BF16)

    back = gather(errors, 1)
    if raw:
        own_unit = unit(errors, y, z)
        out.send(own_unit, unit(errors_mate, y, z), unit_send.at[1], unit_got.at[1], mate)
        for i in range(early, 2 * half // tile):
            send_tile(down_hbm, 1, i)
    back.run()

    def slopes(group, errors, down, pre, slope_in):
        block = every if group is None else group_rows(group)

        def finish(cols, values):
            slope_in[block, cols] = (scale_down * values * silu_slope(pre[block, cols])).astype(BF16)

        contract(block, errors, down, True, finish)

    def both(body):
        body(None)

    def turn(hidden, slots):
        def step(j, carry):
            rows = pl.ds(pl.multiple_of(j * LANES, 16), LANES)
            hidden_t[rows, :] = hidden[:, lanes(j, LANES)].T
            return carry

        def step_slots(j, carry):
            blocks = half // LANES
            rows = pl.ds(pl.multiple_of(j * LANES, 16), LANES)
            slots_t[rows, :] = slots[j // blocks, :, lanes(j % blocks, LANES)].T
            return carry

        lax.fori_loop(0, units // LANES, step, 0)
        lax.fori_loop(0, 2 * half // LANES, step_slots, 0)

    def moved(mat, i, errors, up, down, slope_in):
        if mat == 0:
            rows = pl.ds(pl.multiple_of(i * tile, LANES), tile)
            change = scale_up * jnp.dot(slots_t[rows, :], slope_in[...], preferred_element_type=F32)
            old = tiles(up, 0, i)[...]
        else:
            side, cols = i // (half // tile), lanes(i % (half // tile), tile)
            change = scale_down * jnp.dot(hidden_t[...], errors[side, :, cols], preferred_element_type=F32)
            old = tiles(down, 1, i)[...]
        return (old.astype(F32) - learn_rate * change).astype(BF16)

    own = (errors, up, down, slope_in)
    count = 2 * half // tile

    def every_tile(body, first=0, last=None):
        def step(i, carry):
            for mat in (1, 0):
                body(mat, i)
            return carry

        lax.fori_loop(first, count if last is None else last, step, 0)

    def own_tile(mat, i):
        tiles((up, down)[mat], mat, i)[...] = moved(mat, i, *own)

    def store_of(mat, i):
        ref = (up_mate, down_mate)[mat]
        return pltpu.make_async_copy(
            tiles(ref, mat, i), tiles((up_out, down_out)[mat], mat, i), store_sem.at[mat, i]
        )

    def blend(mat, i, theirs):
        mine = tiles((up, down)[mat], mat, i)[...]
        tiles((up_mate, down_mate)[mat], mat, i)[...] = (
            0.5 * (mine.astype(F32) + theirs.astype(F32))
        ).astype(BF16)
        store_of(mat, i).start()

    if raw:
        arrived(unit(errors_mate, y, z), unit_send.at[1], unit_got.at[1], mate)
        back_mate.open()
        steps = back_mate.steps()
        spread_mate.finish()

        def wait_up(i, carry):
            wait_tile(0, i)
            return carry

        def wait_down(i, carry):
            wait_tile(1, i)
            return carry

        lax.fori_loop(0, count, wait_up, 0)
        for step in steps[:1]:
            step()
        both(lambda group: ahead(group, slots_mate, up_mate, pre_mate, hidden_mate))
        for step in steps[1:3]:
            step()
        back.finish()
        both(lambda group: slopes(group, errors, down, pre, slope_in))
        for step in steps[3:5]:
            step()
        turn(hidden, slots)
        every_tile(own_tile)
        for step in steps[5:]:
            step()
        turn(hidden_mate, slots_mate)
        lax.fori_loop(0, count, wait_down, 0)
        back_mate.finish()
        both(lambda group: slopes(group, errors_mate, down_mate, pre_mate, slope_in))
        theirs = (errors_mate, up_mate, down_mate, slope_in)
        every_tile(lambda mat, i: blend(mat, i, moved(mat, i, *theirs)))
    else:
        turn(hidden, slots)
        back.finish()
        both(lambda group: slopes(group, errors, down, pre, slope_in))

        def move_and_send(mat, i):
            own_tile(mat, i)
            send_tile((up, down)[mat], mat, i)

        def meet(mat, i):
            wait_tile(mat, i)
            blend(mat, i, tiles((up_mate, down_mate)[mat], mat, i)[...])

        every_tile(move_and_send)
        every_tile(meet)

    def settle(mat, i):
        tile_copy((up_hbm, down_hbm)[mat] if raw else (up, down)[mat], mat, i).wait_send()
        store_of(mat, i).wait()

    every_tile(settle)
    out.drain()


def expert(bit, raw, tokens, routes, weights, up, down):
    width = tokens.shape[1]
    units = up.shape[1]
    half = width // 2
    tiles = width // min(TILE, half // 3)
    slot_count = SIDE * SIDE * CAP
    hidden_total = units * SIDE * SIDE
    vmem = pl.BlockSpec(memory_space=pltpu.VMEM)
    hbm = pl.BlockSpec(memory_space=pl.ANY)
    dma = pltpu.SemaphoreType.DMA
    all_rows = pltpu.VMEM((2, slot_count, half), BF16)
    gathers = 4 if raw else 2
    more = []
    if raw:
        more = [
            all_rows,
            all_rows,
            pltpu.VMEM((slot_count, units), BF16),
            pltpu.VMEM((slot_count, units), F32),
            dma((2,)),
            dma((2,)),
        ]
    return pl.pallas_call(
        partial(expert_kernel, bit, raw, width ** (-0.5), hidden_total ** (-0.5)),
        out_shape=(
            jax.ShapeDtypeStruct((width, units), BF16),
            jax.ShapeDtypeStruct((units, width), BF16),
        ),
        in_specs=[vmem, vmem, vmem, hbm, hbm],
        out_specs=(hbm, hbm),
        scratch_shapes=[
            all_rows,
            all_rows,
            pltpu.VMEM((width, units), BF16),
            pltpu.VMEM((units, width), BF16),
            pltpu.VMEM((slot_count, units), F32),
            pltpu.VMEM((slot_count, units), BF16),
            all_rows,
            pltpu.VMEM((2, SIDE, PAIR, half // 2), BF16),
            pltpu.VMEM((2, SIDE, PAIR, half), BF16),
            pltpu.VMEM((SIDE - 1, PAIR, half), BF16),
            pltpu.VMEM((PAIR, half), F32),
            pltpu.VMEM((STAGE, half + LANES), BF16),
            pltpu.VMEM((STAGE, half + LANES), BF16),
            pltpu.VMEM((PAIR, LANES), F32),
            pltpu.VMEM((slot_count, units), BF16),
            pltpu.VMEM((width, units), BF16),
            pltpu.VMEM((units, width), BF16),
            dma((2,)),
            dma((2, tiles)),
            dma((2,)),
            dma((gathers, 22)),
            dma((gathers, SIDE * SIDE)),
            dma((gathers, 3, SIDE * SIDE)),
            dma((30,)),
            dma((2, SIDE)),
            dma((2, SIDE, 2)),
            dma((SIDE - 1,)),
            dma((2, tiles)),
            dma((2, tiles)),
            pltpu.VMEM((units, slot_count), BF16),
            pltpu.VMEM((width, slot_count), BF16),
            pltpu.VMEM((SIDE - 1, PAIR, half // 3), BF16),
            dma((SIDE - 1,)),
        ]
        + more,
        compiler_params=pltpu.CompilerParams(
            collective_id=bit, has_side_effects=True, vmem_limit_bytes=56 * 1024 * 1024
        ),
        cost_estimate=pl.CostEstimate(
            flops=10 * slot_count * width * units, bytes_accessed=200_000_000, transcendentals=2 * slot_count * units
        ),
    )(tokens, routes, weights, up, down)


RAW_BITS = (1, 2)


def on_device(tokens, routing, router_weight, w_up, w_down, step_number):
    levels = lax.axis_size("island").bit_length() - 1
    bit_index = jnp.remainder(step_number[0], jnp.int32(levels))
    new_up, new_down = lax.switch(
        bit_index,
        [partial(expert, bit, bit in RAW_BITS) for bit in range(levels)],
        tokens[0],
        routing[0].T,
        router_weight[0].T,
        w_up[0],
        w_down[0],
    )
    return (new_up[None], new_down[None])


def solution(mesh):
    placed = (
        P("island", "fsdp", None),
        P("island", "fsdp", None),
        P("island", "fsdp", None),
        P("island", None, "fsdp"),
        P("island", "fsdp", None),
        P(),
    )
    return jax.shard_map(
        on_device,
        mesh=mesh,
        in_specs=placed,
        out_specs=(P("island", None, "fsdp"), P("island", "fsdp", None)),
        check_vma=False,
    )
```
